128 devices in a mesh: group: 16 (over x, z), local: 8 (over y, core).
Axes of the slice: x: 4, y: 4, z: 4, core: 2. Of those that a mesh axis runs over, the one named last changes fastest.
Arguments:
- tokens: bfloat16 [16384, 4096], P(('group', 'local')), may hold values from -6 to 6
- expert_ids: int32 [16384, 2], P(('group', 'local')), may hold values from 0 to 63, all different within a row; in each aligned block of 128 rows (0 to 127, 128 to 255, ...) at most 6 rows name the same one
- gate_scores: float32 [16384, 2], P(('group', 'local')), may hold values from 0.1 to 1
- w_gate: bfloat16 [128, 4096, 768], P(('group', 'local')), may hold values from -0.09375 to 0.09375
- w_up: bfloat16 [128, 4096, 768], P(('group', 'local')), may hold values from -0.09375 to 0.09375
- w_down: bfloat16 [128, 768, 4096], P(('group', 'local')), may hold values from -0.15625 to 0.15625
Outputs:
- mixed: bfloat16 [16384, 4096], P(('group', 'local'))
The draws below stay inside these ranges and needn't reach their ends.
Inputs may be any that keep to these rules, and one draw needn't show every extreme that they name: `expert_ids`: among the 128 rows of one device (aligned blocks), each row names 2 different experts, and no expert is named by more than 6 rows of the block; some expert reaches 6 rows.
All inputs are finite; a program needn't handle non-finite values.
Results may differ from the reference program's by a relative error of at most 0.0065.
Values may be sent and summed in bfloat16 or wider, within the bound.
A program may use at most 128 MiB of HBM per device.

```python
import math
import jax
import jax.numpy as jnp
import numpy as np
from jax import lax

D = 4096
FF = 1536
TOP = 2
TOK_DEV = 128
TOKENS = 16384
EXPERTS = 64
CAP = 6


def steps_of(stream_key, extent, pieces, low, largest):
    factor_of = 1.0
    for dim, blocks in pieces:
        heights = jax.random.uniform(jax.random.fold_in(jax.random.fold_in(stream_key, 6), dim), (blocks,), jnp.float32, low / len(pieces), largest / len(pieces))
        factor_of = factor_of * jnp.repeat(jnp.exp(heights), extent[dim] // blocks).reshape((-1,) + (1,) * (len(extent) - 1 - dim))
    return factor_of


def deal_out(own_key, own, number, rows, number_of, top, limit, slope):
    order = jax.random.permutation(own_key, number_of)
    heavy_load, common = portions_of(number_of, rows * top, limit, slope, True), portions_of(number_of, rows * top, limit, slope, False)
    places = jnp.arange(number_of)

    def named(lengths, rotation):
        used = int((lengths > 0).sum())
        fixed = max(1, used // 4)
        shifted = fixed + (places - fixed + rotation * (used - fixed)) % max(1, number_of - fixed)
        return jnp.zeros((number_of,), jnp.int32).at[order[jnp.where(places < fixed, places, shifted)]].set(jnp.asarray(lengths, jnp.int32))

    lengths = jnp.where(number % 4 == 0, named(heavy_load, number // 4), named(common, number - number // 4 - 1))
    mixed = jax.random.permutation(jax.random.fold_in(own, 3), number_of)
    donor, taker = mixed[0:number_of // 2 * 2:2], mixed[1:number_of // 2 * 2:2]
    slack = jnp.minimum(lengths[donor] - 1, limit - lengths[taker]) // 2
    slack = jnp.where((donor == order[0]) | (taker == order[0]) | (lengths[taker] == 0), 0, jnp.maximum(slack, 0))
    shifted = jax.random.randint(jax.random.fold_in(own, 4), (number_of // 2,), 0, 1 << 20) % (slack + 1)
    lengths = lengths.at[donor].add(-shifted).at[taker].add(shifted)
    items = jnp.searchsorted(jnp.cumsum(lengths), jnp.arange(rows * top), side="right").astype(jnp.int32)
    table = items.reshape(top, rows).T
    table = table[jax.random.permutation(jax.random.fold_in(own, 1), rows)]
    rotation = jax.random.randint(jax.random.fold_in(own, 2), (rows, 1), 0, top)
    return jnp.take_along_axis(table, (jnp.arange(top)[None, :] + rotation) % top, axis=1)


def portions_of(amount, total, reach, lean, full):
    portions = [(1 << 20) // math.isqrt(grade ** lean) + 1 for grade in range(1, amount + 1)]
    largest = reach if full else min(reach, max(-(-total // amount), total * portions[0] // sum(portions)))
    least = 1 if total - largest >= amount - 1 else 0
    given, spare = [largest] + [least] * (amount - 1), total - largest - least * (amount - 1)
    while spare > 0:
        candidates = [i for i in range(1, amount) if given[i] < largest] or [i for i in range(1, amount) if given[i] < reach]
        pool, budget = sum([portions[i] for i in candidates]), spare
        for i in candidates:
            more = min(reach - given[i], max(1, budget * portions[i] // pool), spare)
            given[i] = given[i] + more
            spare = spare - more
    return np.array(given)


def centred(stream_key, extent, spread, limit, split=(), held_as=jnp.bfloat16):
    loudness = steps_of(stream_key, extent, split, -0.22, 0.18) if split else 1.0
    entries = jax.random.normal(stream_key, extent, jnp.float32) * spread * loudness
    return jnp.minimum(jnp.maximum(entries, -limit), limit).astype(held_as)


def setup_inputs(seed: int = 0) -> dict:
    streams_of = jax.random.split(jax.random.key(seed), 7)
    tokens = centred(streams_of[0], (TOKENS, D), 1.0, 6.0, ((0, 128),))
    expert_ids_keys = jax.random.split(jax.random.fold_in(streams_of[1], 1), TOKENS // TOK_DEV)
    expert_ids_turns = jax.random.permutation(jax.random.fold_in(streams_of[1], 3), TOKENS // TOK_DEV)
    expert_ids = jax.vmap(lambda own, number: deal_out(jax.random.fold_in(streams_of[1], 2), own, number, TOK_DEV, EXPERTS, TOP, CAP, 2))(expert_ids_keys, expert_ids_turns).reshape((TOKENS, TOP))
    gate_scores = jnp.clip(jnp.exp(math.log(1.0) - 2.3025851 * jax.random.uniform(streams_of[2], (TOKENS, TOP), jnp.float32) ** steps_of(streams_of[2], (TOKENS, TOP), ((0, 128),), -0.2, 0.2)), 0.1, 1.0)
    w_gate = centred(streams_of[3], (2 * EXPERTS, D, FF // 2), D ** -0.5, 0.09375, ((0, 128),))
    w_up = centred(streams_of[4], (2 * EXPERTS, D, FF // 2), D ** -0.5, 0.09375, ((0, 128),))
    w_down = centred(streams_of[5], (2 * EXPERTS, FF // 2, D), FF ** -0.5, 0.15625, ((0, 128),))
    return {"tokens": tokens, "expert_ids": expert_ids, "gate_scores": gate_scores, "w_gate": w_gate, "w_up": w_up, "w_down": w_down}


def reference(tokens, expert_ids, gate_scores, w_gate, w_up, w_down):
    total = tokens.shape[0]
    top = expert_ids.shape[1]
    width = tokens.shape[1]
    assigned = total * top
    block_rows = 128
    weights = gate_scores / jnp.sum(gate_scores, axis=1, keepdims=True)
    flat_ids = expert_ids.reshape(-1).astype(jnp.int32)
    order = jnp.argsort(flat_ids, stable=True).astype(jnp.int32)
    expert_range = jnp.arange(EXPERTS, dtype=jnp.int32)
    counts = jnp.sum((flat_ids[:, None] == expert_range[None, :]).astype(jnp.int32), axis=0)
    starts = jnp.cumsum(counts) - counts
    tiles_per = (counts + block_rows - 1) // block_rows
    tile_start = jnp.cumsum(tiles_per) - tiles_per
    tile_end = tile_start + tiles_per
    num_tiles = assigned // block_rows + EXPERTS

    def one_tile(tile):
        expert = jnp.minimum(jnp.sum((tile_end <= tile).astype(jnp.int32)), EXPERTS - 1).astype(jnp.int32)
        within = tile - tile_start[expert]
        offsets = within * block_rows + jnp.arange(block_rows, dtype=jnp.int32)
        valid = offsets < counts[expert]
        position = jnp.minimum(starts[expert] + offsets, assigned - 1).astype(jnp.int32)
        who = order[position]
        rows = tokens[who // top]
        total_part = jnp.zeros((block_rows, width), jnp.float32)
        for half in range(2):
            index = 2 * expert + half
            gate = jnp.dot(rows, w_gate[index], preferred_element_type=jnp.float32)
            upper = jnp.dot(rows, w_up[index], preferred_element_type=jnp.float32)
            hidden = (jax.nn.silu(gate) * upper).astype(jnp.bfloat16)
            part = jnp.dot(hidden, w_down[index], preferred_element_type=jnp.float32).astype(jnp.bfloat16)
            part = lax.optimization_barrier(part)
            total_part = total_part + part.astype(jnp.float32)
        result = total_part.astype(jnp.bfloat16)
        return result, jnp.where(valid, who, assigned).astype(jnp.int32)

    outputs, owners = lax.map(one_tile, jnp.arange(num_tiles, dtype=jnp.int32))
    table = jnp.zeros((assigned + 1, width), jnp.bfloat16)
    table = table.at[owners.reshape(-1)].set(outputs.reshape(-1, width))
    table = lax.optimization_barrier(table)
    picked = table[:assigned].reshape(total, top, width).astype(jnp.float32)
    mixed = jnp.sum(picked * weights[:, :, None], axis=1)
    return mixed.astype(jnp.bfloat16)
```

```python
import jax
import jax.numpy as jnp
from jax import lax
from jax.experimental import pallas as pl
from jax.experimental.pallas import tpu as pltpu
from jax.sharding import PartitionSpec as P

MESH = pl.DeviceIdType.MESH
BF16, F32 = jnp.bfloat16, jnp.float32

SIDE = 4
CHIPS = SIDE**3
CAP = 6
GROUPS = 4
SLOTS = CHIPS // GROUPS
CHUNK = 512
PIECES = 8
PAIRS = CAP // 2
LANES = PAIRS * CHUNK
OWN = SLOTS * CAP
STRIDE = 22


def shift_of(slot):
    return 1 + lax.rem(slot * STRIDE, CHIPS - 1)


def kernel(
    ids, scores, tok_hbm, gate_hbm, up_hbm, down_hbm, out,
    tok, w_gate, w_up, w_down,
    sent, got, rows, hidden, part_own, part_out, part_in, answer, back,
    pick, mixing, spread, unspread, stage, flat, total,
    load_sem, there_send, there_recv, row_send, row_recv, part_send, part_recv, back_send, back_recv, own_sem,
):
    group, local = lax.axis_index("group"), lax.axis_index("local")
    x, z = lax.div(group, SIDE), lax.rem(group, SIDE)
    y, core = lax.div(local, 2), lax.rem(local, 2)
    twin = (group, local + 1 - 2 * core)

    def partner(slot, sign):
        shift = shift_of(slot)
        far_x = lax.rem(x + SIDE + sign * lax.div(shift, SIDE * SIDE), SIDE)
        far_y = lax.rem(y + SIDE + sign * lax.rem(lax.div(shift, SIDE), SIDE), SIDE)
        far_z = lax.rem(z + SIDE + sign * lax.rem(shift, SIDE), SIDE)
        return (far_x * SIDE + far_z, far_y * 2 + core)

    def loads():
        pairs = ((tok_hbm, tok), (gate_hbm.at[0], w_gate), (up_hbm.at[0], w_up), (down_hbm.at[0], w_down))
        return [pltpu.make_async_copy(a, b, load_sem.at[n]) for n, (a, b) in enumerate(pairs)]

    barrier = pltpu.get_barrier_semaphore()

    def greet(slot, carry):
        pl.semaphore_signal(barrier, inc=1, device_id=partner(slot, 1), device_id_type=MESH)
        return carry

    lax.fori_loop(0, CHIPS - 1, greet, 0)
    pl.semaphore_signal(barrier, inc=1, device_id=twin, device_id_type=MESH)
    for copy in loads():
        copy.start()

    n = 2 * CHIPS
    row = lax.broadcasted_iota(jnp.int32, (n, n), 0)
    column = lax.broadcasted_iota(jnp.int32, (n, n), 1)
    slot, odd = lax.shift_right_logical(row, 1), row & 1
    shift = jnp.where(slot == CHIPS - 1, 0, shift_of(slot))
    expert = ((x + lax.shift_right_logical(shift, 4)) & 3) * 16 + ((z + shift) & 3) * 4 + ((y + lax.shift_right_logical(shift, 2)) & 3)
    first, second = expert == ids[0:1, :], expert == ids[1:2, :]
    chosen = jnp.where(first | second, 1.0, 0.0)
    earlier = jnp.where(row < column, 1.0, 0.0).astype(BF16)
    rank = jnp.dot(chosen.astype(BF16), earlier, preferred_element_type=F32)
    scale = scores[0:1, :] + scores[1:2, :]
    weight = jnp.where(first, scores[0:1, :] / scale, 0.0) + jnp.where(second, scores[1:2, :] / scale, 0.0)
    for j in range(PAIRS):
        here = jnp.where(rank == (2 * j + odd).astype(F32), chosen, 0.0)
        high = (here * weight).astype(BF16)
        low = (here * weight - high.astype(F32)).astype(BF16)
        for q in range(GROUPS):
            part = slice(2 * SLOTS * q, 2 * SLOTS * (q + 1))
            place = slice(2 * SLOTS * j, 2 * SLOTS * (j + 1))
            pick[q, place, :] = here[part].astype(BF16)
            mixing[0, q, place, :] = high[part]
            mixing[1, q, place, :] = low[part]

    m = 2 * SLOTS * PIECES
    a = lax.broadcasted_iota(jnp.int32, (m, m), 0)
    b = lax.broadcasted_iota(jnp.int32, (m, m), 1)

    def meets(a, b):
        same = (lax.shift_right_logical(a, 4) == (lax.shift_right_logical(b, 1) & 15)) & ((lax.shift_right_logical(a, 1) & 7) == lax.shift_right_logical(b, 5)) & ((a & 1) == (b & 1))
        return jnp.where(same, 1.0, 0.0).astype(BF16)

    spread[...] = meets(a, b)
    unspread[...] = meets(b, a)

    def pack(target, q):
        for j in range(PAIRS):
            lane = slice(j * CHUNK, (j + 1) * CHUNK)
            block = jnp.dot(spread[...], stage[:, lane], preferred_element_type=F32).astype(BF16)
            target[pl.ds(q * SLOTS, SLOTS), :, lane] = block.reshape(SLOTS, 2 * PIECES, CHUNK)

    def unpack(source, q, put):
        for j in range(PAIRS):
            lane = slice(j * CHUNK, (j + 1) * CHUNK)
            block = source[pl.ds(q * SLOTS, SLOTS), :, lane].reshape(m, CHUNK)
            block = jnp.dot(unspread[...], block, preferred_element_type=F32).astype(BF16)
            for c in range(PIECES):
                put(slice(2 * SLOTS * j, 2 * SLOTS * (j + 1)), slice(c * CHUNK, (c + 1) * CHUNK), block[2 * SLOTS * c : 2 * SLOTS * (c + 1)])

    def to_stage(c, value):
        for j in range(PAIRS):
            stage[2 * SLOTS * c : 2 * SLOTS * (c + 1), j * CHUNK : (j + 1) * CHUNK] = value[2 * SLOTS * j : 2 * SLOTS * (j + 1)]

    def remote(source, target, slot, sign, send, recv):
        return pltpu.make_async_remote_copy(
            src_ref=source.at[slot], dst_ref=target.at[slot], send_sem=send, recv_sem=recv,
            device_id=partner(slot, sign), device_id_type=MESH,
        )

    def send_group(source, target, q, sign, send, recv):
        def one(i, carry):
            remote(source, target, q * SLOTS + i, sign, send, recv.at[q]).start()
            return carry

        lax.fori_loop(0, SLOTS - lax.div(q, GROUPS - 1), one, 0)

        @pl.when(q == GROUPS - 1)
        def _():
            pltpu.make_async_copy(source.at[CHIPS - 1], target.at[CHIPS - 1], own_sem).start()

    def wait_group(target, q, recv):
        @pl.when(q < GROUPS - 1)
        def _():
            ref = target.at[pl.ds(0, SLOTS)]
            pltpu.make_async_copy(ref, ref, recv.at[q]).wait()

        @pl.when(q == GROUPS - 1)
        def _():
            ref = target.at[pl.ds(0, SLOTS - 1)]
            pltpu.make_async_copy(ref, ref, recv.at[q]).wait()
            pltpu.make_async_copy(target.at[CHIPS - 1], target.at[CHIPS - 1], own_sem).wait()

    loads()[0].wait()
    pl.semaphore_wait(barrier, CHIPS)

    def dispatch(q, carry):
        for c in range(PIECES):
            value = jnp.dot(pick[q], tok[:, c * CHUNK : (c + 1) * CHUNK], preferred_element_type=F32)
            to_stage(c, value.astype(BF16))
        pack(sent, q)
        send_group(sent, got, q, 1, there_send, there_recv)
        return carry

    lax.fori_loop(0, GROUPS, dispatch, 0)
    for copy in loads()[1:]:
        copy.wait()

    def to_twin(source, target, send, recv):
        return pltpu.make_async_remote_copy(
            src_ref=source, dst_ref=target, send_sem=send, recv_sem=recv, device_id=twin, device_id_type=MESH
        )

    def work(q, carry):
        wait_group(got, q, there_recv)

        def put(r, c, value):
            rows[q, r, c] = value

        unpack(got, q, put)
        over = to_twin(rows.at[q, pl.ds(0, OWN)], rows.at[q, pl.ds(OWN, OWN)], row_send.at[q], row_recv.at[q])
        over.start()
        over.wait()

        def up(t, carry):
            lane = pl.ds(pl.multiple_of(t * 256, 256), 256)
            gate = jnp.dot(rows[q], w_gate[:, lane], preferred_element_type=F32)
            upper = jnp.dot(rows[q], w_up[:, lane], preferred_element_type=F32)
            hidden[:, lane] = (gate / (1.0 + jnp.exp(-gate)) * upper).astype(BF16)
            return carry

        lax.fori_loop(0, 3, up, 0)

        def down(t, carry):
            lane = pl.ds(pl.multiple_of(t * CHUNK, CHUNK), CHUNK)
            part = jnp.dot(hidden[...], w_down[:, lane], preferred_element_type=F32).astype(BF16)
            part_own[:, lane] = part[:OWN]
            part_out[q, :, lane] = part[OWN:]
            return carry

        lax.fori_loop(0, PIECES, down, 0)
        over = to_twin(part_out.at[q], part_in.at[q], part_send.at[q], part_recv.at[q])
        over.start()
        over.wait()
        for c in range(PIECES):
            lane = slice(c * CHUNK, (c + 1) * CHUNK)
            to_stage(c, (part_own[:, lane].astype(F32) + part_in[q, :, lane].astype(F32)).astype(BF16))
        pack(answer, q)
        send_group(answer, back, q, -1, back_send, back_recv)
        return carry

    lax.fori_loop(0, GROUPS, work, 0)

    total[...] = jnp.zeros_like(total)

    def finish(q, carry):
        wait_group(back, q, back_recv)

        def put(r, c, value):
            flat[r, c] = value

        unpack(back, q, put)
        for c in range(PIECES):
            lane = slice(c * CHUNK, (c + 1) * CHUNK)
            for h in range(2):
                total[:, lane] += lax.dot_general(mixing[h, q], flat[:, lane], (((0,), (0,)), ((), ())), preferred_element_type=F32)
        return carry

    lax.fori_loop(0, GROUPS, finish, 0)
    out[...] = total[...].astype(BF16)
    for source, send in ((sent, there_send), (answer, back_send)):
        ref = source.at[pl.ds(0, CHIPS - 1)]
        pltpu.make_async_copy(ref, ref, send).wait()


def body(tokens, expert_ids, gate_scores, w_gate, w_up, w_down):
    rows, width = tokens.shape
    half = w_gate.shape[2]
    blocks = (CHIPS, 2 * PIECES, LANES)
    m = 2 * SLOTS * PIECES
    vmem, hbm = pl.BlockSpec(memory_space=pltpu.VMEM), pl.BlockSpec(memory_space=pl.ANY)
    dma = pltpu.SemaphoreType.DMA
    return pl.pallas_call(
        kernel,
        out_shape=jax.ShapeDtypeStruct((rows, width), BF16),
        in_specs=[vmem, vmem, hbm, hbm, hbm, hbm],
        out_specs=vmem,
        scratch_shapes=[
            pltpu.VMEM((rows, width), BF16),
            pltpu.VMEM((width, half), BF16),
            pltpu.VMEM((width, half), BF16),
            pltpu.VMEM((half, width), BF16),
            pltpu.VMEM(blocks, BF16),
            pltpu.VMEM(blocks, BF16),
            pltpu.VMEM((GROUPS, 2 * OWN, width), BF16),
            pltpu.VMEM((2 * OWN, half), BF16),
            pltpu.VMEM((OWN, width), BF16),
            pltpu.VMEM((GROUPS, OWN, width), BF16),
            pltpu.VMEM((GROUPS, OWN, width), BF16),
            pltpu.VMEM(blocks, BF16),
            pltpu.VMEM(blocks, BF16),
            pltpu.VMEM((GROUPS, OWN, rows), BF16),
            pltpu.VMEM((2, GROUPS, OWN, rows), BF16),
            pltpu.VMEM((m, m), BF16),
            pltpu.VMEM((m, m), BF16),
            pltpu.VMEM((m, LANES), BF16),
            pltpu.VMEM((OWN, width), BF16),
            pltpu.VMEM((rows, width), F32),
            dma((4,)),
            dma, dma((GROUPS,)),
            dma((GROUPS,)), dma((GROUPS,)),
            dma((GROUPS,)), dma((GROUPS,)),
            dma, dma((GROUPS,)),
            dma,
        ],
        compiler_params=pltpu.CompilerParams(collective_id=0, has_side_effects=True, vmem_limit_bytes=60 << 20),
    )(expert_ids.T, gate_scores.T, tokens, w_gate, w_up, w_down)


def solution(mesh):
    split = ("group", "local")
    flat, deep = P(split, None), P(split, None, None)
    return jax.shard_map(
        body, mesh=mesh, in_specs=(flat, flat, flat, deep, deep, deep), out_specs=flat, check_vma=False
    )
```

```python
import jax
import jax.numpy as jnp
from jax import lax
from jax.experimental import pallas as pl
from jax.experimental.pallas import tpu as pltpu
from jax.sharding import PartitionSpec as P

MESH = pl.DeviceIdType.MESH
BF16, F32 = jnp.bfloat16, jnp.float32

SIDE = 4
CHIPS = SIDE**3
CAP = 6
GROUPS = 4
SLOTS = CHIPS // GROUPS
CHUNK = 512
PIECES = 8
PAIRS = CAP // 2
LANES = PAIRS * CHUNK
HALF = PIECES // 2 * CHUNK
OWN = SLOTS * CAP
STRIDE = 22
EARLY = 1


def shift_of(slot):
    return 1 + lax.rem((slot + EARLY) * STRIDE, CHIPS - 1)


def kernel(
    ids, scores, tok_hbm, gate_hbm, up_hbm, down_hbm, out,
    tok, w_gate, w_up, w_down,
    sent, got, rows, hidden, part_own, part_out, part_in, answer, back,
    pick, mixing, spread, unspread, stage, flat, total,
    load_sem, there_send, there_recv, row_send, row_recv, part_send, part_recv, back_send, back_recv, own_sem,
):
    group, local = lax.axis_index("group"), lax.axis_index("local")
    x, z = lax.div(group, SIDE), lax.rem(group, SIDE)
    y, core = lax.div(local, 2), lax.rem(local, 2)
    twin = (group, local + 1 - 2 * core)

    def partner(slot, sign):
        shift = shift_of(slot)
        far_x = lax.rem(x + SIDE + sign * lax.div(shift, SIDE * SIDE), SIDE)
        far_y = lax.rem(y + SIDE + sign * lax.rem(lax.div(shift, SIDE), SIDE), SIDE)
        far_z = lax.rem(z + SIDE + sign * lax.rem(shift, SIDE), SIDE)
        return (far_x * SIDE + far_z, far_y * 2 + core)

    def loads():
        pairs = ((tok_hbm, tok), (gate_hbm.at[0], w_gate), (up_hbm.at[0], w_up), (down_hbm.at[0], w_down))
        return [pltpu.make_async_copy(a, b, load_sem.at[n]) for n, (a, b) in enumerate(pairs)]

    barrier = pltpu.get_barrier_semaphore()

    def greet(slot, carry):
        pl.semaphore_signal(barrier, inc=1, device_id=partner(slot, 1), device_id_type=MESH)
        return carry

    loads()[0].start()
    lax.fori_loop(0, CHIPS - 1, greet, 0)
    pl.semaphore_signal(barrier, inc=1, device_id=twin, device_id_type=MESH)
    for copy in loads()[1:]:
        copy.start()

    n = 2 * CHIPS
    row = lax.broadcasted_iota(jnp.int32, (n, n), 0)
    column = lax.broadcasted_iota(jnp.int32, (n, n), 1)
    slot, odd = lax.shift_right_logical(row, 1), row & 1
    shift = jnp.where(slot == CHIPS - 1, 0, shift_of(slot))
    expert = ((x + lax.shift_right_logical(shift, 4)) & 3) * 16 + ((z + shift) & 3) * 4 + ((y + lax.shift_right_logical(shift, 2)) & 3)
    first, second = expert == ids[0:1, :], expert == ids[1:2, :]
    chosen = jnp.where(first | second, 1.0, 0.0)
    earlier = jnp.where(row < column, 1.0, 0.0).astype(BF16)
    rank = jnp.dot(chosen.astype(BF16), earlier, preferred_element_type=F32)
    scale = scores[0:1, :] + scores[1:2, :]
    weight = jnp.where(first, scores[0:1, :] / scale, 0.0) + jnp.where(second, scores[1:2, :] / scale, 0.0)
    for j in range(PAIRS):
        here = jnp.where(rank == (2 * j + odd).astype(F32), chosen, 0.0)
        high = (here * weight).astype(BF16)
        low = (here * weight - high.astype(F32)).astype(BF16)
        for q in range(GROUPS):
            part = slice(2 * SLOTS * q, 2 * SLOTS * (q + 1))
            place = slice(2 * SLOTS * j, 2 * SLOTS * (j + 1))
            pick[q, place, :] = here[part].astype(BF16)
            mixing[0, q, place, :] = high[part]
            mixing[1, q, place, :] = low[part]

    m = 2 * SLOTS * PIECES
    a = lax.broadcasted_iota(jnp.int32, (m, m), 0)
    b = lax.broadcasted_iota(jnp.int32, (m, m), 1)

    def meets(a, b):
        same = (lax.shift_right_logical(a, 4) == (lax.shift_right_logical(b, 1) & 15)) & ((lax.shift_right_logical(a, 1) & 7) == lax.shift_right_logical(b, 5)) & ((a & 1) == (b & 1))
        return jnp.where(same, 1.0, 0.0).astype(BF16)

    spread[...] = meets(a, b)
    unspread[...] = meets(b, a)

    def pack(target, q):
        for j in range(PAIRS):
            lane = slice(j * CHUNK, (j + 1) * CHUNK)
            block = jnp.dot(spread[...], stage[:, lane], preferred_element_type=F32).astype(BF16)
            target[pl.ds(q * SLOTS, SLOTS), :, lane] = block.reshape(SLOTS, 2 * PIECES, CHUNK)

    def unpack(source, q, put):
        for j in range(PAIRS):
            lane = slice(j * CHUNK, (j + 1) * CHUNK)
            block = source[pl.ds(q * SLOTS, SLOTS), :, lane].reshape(m, CHUNK)
            block = jnp.dot(unspread[...], block, preferred_element_type=F32).astype(BF16)
            for c in range(PIECES):
                put(slice(2 * SLOTS * j, 2 * SLOTS * (j + 1)), slice(c * CHUNK, (c + 1) * CHUNK), block[2 * SLOTS * c : 2 * SLOTS * (c + 1)])

    def to_stage(c, value):
        for j in range(PAIRS):
            stage[2 * SLOTS * c : 2 * SLOTS * (c + 1), j * CHUNK : (j + 1) * CHUNK] = value[2 * SLOTS * j : 2 * SLOTS * (j + 1)]

    def remote(source, target, slot, sign, send, recv):
        return pltpu.make_async_remote_copy(
            src_ref=source.at[slot], dst_ref=target.at[slot], send_sem=send, recv_sem=recv,
            device_id=partner(slot, sign), device_id_type=MESH,
        )

    def send_some(source, target, q, start, stop, sign, send, recv):
        def one(i, carry):
            remote(source, target, q * SLOTS + i, sign, send, recv.at[q]).start()
            return carry

        lax.fori_loop(start, stop, one, 0)

    def keep_own(source, target):
        pltpu.make_async_copy(source.at[CHIPS - 1], target.at[CHIPS - 1], own_sem).start()

    def send_group(source, target, q, sign, send, recv):
        send_some(source, target, q, 0, SLOTS - lax.div(q, GROUPS - 1), sign, send, recv)

        @pl.when(q == GROUPS - 1)
        def _():
            keep_own(source, target)

    def wait_group(target, q, recv):
        @pl.when(q < GROUPS - 1)
        def _():
            ref = target.at[pl.ds(0, SLOTS)]
            pltpu.make_async_copy(ref, ref, recv.at[q]).wait()

        @pl.when(q == GROUPS - 1)
        def _():
            ref = target.at[pl.ds(0, SLOTS - 1)]
            pltpu.make_async_copy(ref, ref, recv.at[q]).wait()
            pltpu.make_async_copy(target.at[CHIPS - 1], target.at[CHIPS - 1], own_sem).wait()

    loads()[0].wait()
    pl.semaphore_wait(barrier, CHIPS)

    def dispatch(t, carry):
        q = lax.rem(t + GROUPS - 1, GROUPS)
        for c in range(PIECES):
            value = jnp.dot(pick[q], tok[:, c * CHUNK : (c + 1) * CHUNK], preferred_element_type=F32)
            to_stage(c, value.astype(BF16))
        pack(sent, q)
        start = jnp.where(t == 0, SLOTS - 1 - EARLY, 0)
        send_some(sent, got, q, start, jnp.where(t == 0, SLOTS - 1, SLOTS), 1, there_send, there_recv)
        return carry

    lax.fori_loop(0, GROUPS, dispatch, 0)
    send_some(sent, got, GROUPS - 1, 0, SLOTS - 1 - EARLY, 1, there_send, there_recv)
    keep_own(sent, got)
    for copy in loads()[1:]:
        copy.wait()

    def to_twin(source, target, send, recv):
        return pltpu.make_async_remote_copy(
            src_ref=source, dst_ref=target, send_sem=send, recv_sem=recv, device_id=twin, device_id_type=MESH
        )

    def over_rows(q):
        return to_twin(rows.at[q, pl.ds(0, OWN)], rows.at[q, pl.ds(OWN, OWN)], row_send.at[q], row_recv.at[q])

    def over_part(q, h):
        side = pl.ds(h * HALF, HALF)
        return to_twin(part_out.at[q, :, side], part_in.at[q, :, side], part_send.at[2 * q + h], part_recv.at[2 * q + h])

    def arrive(q):
        wait_group(got, q, there_recv)

        def put(r, c, value):
            rows[q, r, c] = value

        unpack(got, q, put)
        over_rows(q).start()

    arrive(0)

    def work(q, carry):
        over_rows(q).wait_recv()

        def up(t, carry):
            lane = pl.ds(pl.multiple_of(t * 256, 256), 256)
            gate = jnp.dot(rows[q], w_gate[:, lane], preferred_element_type=F32)
            upper = jnp.dot(rows[q], w_up[:, lane], preferred_element_type=F32)
            hidden[:, lane] = (gate / (1.0 + jnp.exp(-gate)) * upper).astype(BF16)
            return carry

        lax.fori_loop(0, 3, up, 0)

        for h in range(2):
            def down(t, carry):
                lane = pl.ds(pl.multiple_of(h * HALF + t * CHUNK, CHUNK), CHUNK)
                part = jnp.dot(hidden[...], w_down[:, lane], preferred_element_type=F32).astype(BF16)
                part_own[:, lane] = part[:OWN]
                part_out[q, :, lane] = part[OWN:]
                return carry

            lax.fori_loop(0, PIECES // 2, down, 0)
            over_part(q, h).start()

        @pl.when(q < GROUPS - 1)
        def _():
            arrive(q + 1)

        for c in range(PIECES):
            if c % (PIECES // 2) == 0:
                over_part(q, c // (PIECES // 2)).wait_recv()
            lane = slice(c * CHUNK, (c + 1) * CHUNK)
            to_stage(c, (part_own[:, lane].astype(F32) + part_in[q, :, lane].astype(F32)).astype(BF16))
        pack(answer, q)
        send_group(answer, back, q, -1, back_send, back_recv)
        return carry

    lax.fori_loop(0, GROUPS, work, 0)

    total[...] = jnp.zeros_like(total)

    def finish(q, carry):
        wait_group(back, q, back_recv)

        def put(r, c, value):
            flat[r, c] = value

        unpack(back, q, put)
        for c in range(PIECES):
            lane = slice(c * CHUNK, (c + 1) * CHUNK)
            for h in range(2):
                total[:, lane] += lax.dot_general(mixing[h, q], flat[:, lane], (((0,), (0,)), ((), ())), preferred_element_type=F32)
        return carry

    lax.fori_loop(0, GROUPS, finish, 0)
    out[...] = total[...].astype(BF16)
    for q in range(GROUPS):
        over_rows(q).wait_send()
        for h in range(2):
            over_part(q, h).wait_send()
    for source, send in ((sent, there_send), (answer, back_send)):
        ref = source.at[pl.ds(0, CHIPS - 1)]
        pltpu.make_async_copy(ref, ref, send).wait()


def body(tokens, expert_ids, gate_scores, w_gate, w_up, w_down):
    rows, width = tokens.shape
    half = w_gate.shape[2]
    blocks = (CHIPS, 2 * PIECES, LANES)
    m = 2 * SLOTS * PIECES
    vmem, hbm = pl.BlockSpec(memory_space=pltpu.VMEM), pl.BlockSpec(memory_space=pl.ANY)
    dma = pltpu.SemaphoreType.DMA
    return pl.pallas_call(
        kernel,
        out_shape=jax.ShapeDtypeStruct((rows, width), BF16),
        in_specs=[vmem, vmem, hbm, hbm, hbm, hbm],
        out_specs=vmem,
        scratch_shapes=[
            pltpu.VMEM((rows, width), BF16),
            pltpu.VMEM((width, half), BF16),
            pltpu.VMEM((width, half), BF16),
            pltpu.VMEM((half, width), BF16),
            pltpu.VMEM(blocks, BF16),
            pltpu.VMEM(blocks, BF16),
            pltpu.VMEM((GROUPS, 2 * OWN, width), BF16),
            pltpu.VMEM((2 * OWN, half), BF16),
            pltpu.VMEM((OWN, width), BF16),
            pltpu.VMEM((GROUPS, OWN, width), BF16),
            pltpu.VMEM((GROUPS, OWN, width), BF16),
            pltpu.VMEM(blocks, BF16),
            pltpu.VMEM(blocks, BF16),
            pltpu.VMEM((GROUPS, OWN, rows), BF16),
            pltpu.VMEM((2, GROUPS, OWN, rows), BF16),
            pltpu.VMEM((m, m), BF16),
            pltpu.VMEM((m, m), BF16),
            pltpu.VMEM((m, LANES), BF16),
            pltpu.VMEM((OWN, width), BF16),
            pltpu.VMEM((rows, width), F32),
            dma((4,)),
            dma, dma((GROUPS,)),
            dma((GROUPS,)), dma((GROUPS,)),
            dma((2 * GROUPS,)), dma((2 * GROUPS,)),
            dma, dma((GROUPS,)),
            dma,
        ],
        compiler_params=pltpu.CompilerParams(collective_id=0, has_side_effects=True, vmem_limit_bytes=52 << 20),
    )(expert_ids.T, gate_scores.T, tokens, w_gate, w_up, w_down)


def solution(mesh):
    split = ("group", "local")
    flat, deep = P(split, None), P(split, None, None)
    return jax.shard_map(
        body, mesh=mesh, in_specs=(flat, flat, flat, deep, deep, deep), out_specs=flat, check_vma=False
    )
```

```python
import jax
import jax.numpy as jnp
from jax import lax
from jax.experimental import pallas as pl
from jax.experimental.pallas import tpu as pltpu
from jax.sharding import PartitionSpec as P

MESH = pl.DeviceIdType.MESH
BF16, F32 = jnp.bfloat16, jnp.float32

SIDE = 4
CHIPS = SIDE**3
CAP = 6
GROUPS = 4
SLOTS = CHIPS // GROUPS
CHUNK = 512
PIECES = 8
PAIRS = CAP // 2
LANES = PAIRS * CHUNK
HALF = PIECES // 2 * CHUNK
OWN = SLOTS * CAP
STRIDE = 13
EARLY = 1


def shift_of(slot):
    return 1 + lax.rem((slot + EARLY) * STRIDE, CHIPS - 1)


def kernel(
    ids_hbm, scores_hbm, tok_hbm, gate_hbm, up_hbm, down_hbm, out,
    ids, scores, tok, w_gate, w_up, w_down,
    sent, got, rows, hidden, part_own, part_out, part_in, answer, back,
    pick, mixing, spread, unspread, stage, flat, total,
    load_sem, there_send, there_recv, row_send, row_recv, part_send, part_recv, back_send, back_recv, own_sem,
):
    group, local = lax.axis_index("group"), lax.axis_index("local")
    x, z = lax.div(group, SIDE), lax.rem(group, SIDE)
    y, core = lax.div(local, 2), lax.rem(local, 2)
    twin = (group, local + 1 - 2 * core)

    def partner(slot, sign):
        shift = shift_of(slot)
        far_x = lax.rem(x + SIDE + sign * lax.div(shift, SIDE * SIDE), SIDE)
        far_y = lax.rem(y + SIDE + sign * lax.rem(lax.div(shift, SIDE), SIDE), SIDE)
        far_z = lax.rem(z + SIDE + sign * lax.rem(shift, SIDE), SIDE)
        return (far_x * SIDE + far_z, far_y * 2 + core)

    def loads():
        pairs = (
            (ids_hbm, ids), (scores_hbm, scores), (tok_hbm, tok),
            (gate_hbm.at[0], w_gate), (up_hbm.at[0], w_up), (down_hbm.at[0], w_down),
        )
        return [pltpu.make_async_copy(a, b, load_sem.at[n]) for n, (a, b) in enumerate(pairs)]

    barrier = pltpu.get_barrier_semaphore()

    for copy in loads()[:3]:
        copy.start()
    along = [[lax.rem(v + d, SIDE) for d in range(SIDE)] for v in (x, y, z)]
    for dx in (2, 1, 3, 0):
        for dz in (2, 1, 3, 0):
            wide = along[0][dx] * SIDE + along[2][dz]
            for dy in (2, 1, 3, 0):
                if dx or dy or dz:
                    pl.semaphore_signal(barrier, inc=1, device_id=(wide, along[1][dy] * 2 + core), device_id_type=MESH)
    pl.semaphore_signal(barrier, inc=1, device_id=twin, device_id_type=MESH)
    for copy in loads()[3:]:
        copy.start()
    for copy in loads()[:2]:
        copy.wait()

    n = 2 * CHIPS
    row = lax.broadcasted_iota(jnp.int32, (n, n), 0)
    column = lax.broadcasted_iota(jnp.int32, (n, n), 1)
    slot, odd = lax.shift_right_logical(row, 1), row & 1
    shift = jnp.where(slot == CHIPS - 1, 0, shift_of(slot))
    expert = ((x + lax.shift_right_logical(shift, 4)) & 3) * 16 + ((z + shift) & 3) * 4 + ((y + lax.shift_right_logical(shift, 2)) & 3)
    first, second = expert == ids[0:1, :], expert == ids[1:2, :]
    chosen = jnp.where(first | second, 1.0, 0.0)
    earlier = jnp.where(row < column, 1.0, 0.0).astype(BF16)
    rank = jnp.dot(chosen.astype(BF16), earlier, preferred_element_type=F32)
    scale = scores[0:1, :] + scores[1:2, :]
    weight = jnp.where(first, scores[0:1, :] / scale, 0.0) + jnp.where(second, scores[1:2, :] / scale, 0.0)
    for j in range(PAIRS):
        here = jnp.where(rank == (2 * j + odd).astype(F32), chosen, 0.0)
        high = (here * weight).astype(BF16)
        low = (here * weight - high.astype(F32)).astype(BF16)
        for q in range(GROUPS):
            part = slice(2 * SLOTS * q, 2 * SLOTS * (q + 1))
            place = slice(2 * SLOTS * j, 2 * SLOTS * (j + 1))
            pick[q, place, :] = here[part].astype(BF16)
            mixing[0, q, place, :] = high[part]
            mixing[1, q, place, :] = low[part]

    m = 2 * SLOTS * PIECES
    a = lax.broadcasted_iota(jnp.int32, (m, m), 0)
    b = lax.broadcasted_iota(jnp.int32, (m, m), 1)

    def meets(a, b):
        same = (lax.shift_right_logical(a, 4) == (lax.shift_right_logical(b, 1) & 15)) & ((lax.shift_right_logical(a, 1) & 7) == lax.shift_right_logical(b, 5)) & ((a & 1) == (b & 1))
        return jnp.where(same, 1.0, 0.0).astype(BF16)

    spread[...] = meets(a, b)
    unspread[...] = meets(b, a)

    def pack(target, q):
        for j in range(PAIRS):
            lane = slice(j * CHUNK, (j + 1) * CHUNK)
            block = jnp.dot(spread[...], stage[:, lane], preferred_element_type=F32).astype(BF16)
            target[pl.ds(q * SLOTS, SLOTS), :, lane] = block.reshape(SLOTS, 2 * PIECES, CHUNK)

    def unpack(source, q, put):
        for j in range(PAIRS):
            lane = slice(j * CHUNK, (j + 1) * CHUNK)
            block = source[pl.ds(q * SLOTS, SLOTS), :, lane].reshape(m, CHUNK)
            block = jnp.dot(unspread[...], block, preferred_element_type=F32).astype(BF16)
            for c in range(PIECES):
                put(slice(2 * SLOTS * j, 2 * SLOTS * (j + 1)), slice(c * CHUNK, (c + 1) * CHUNK), block[2 * SLOTS * c : 2 * SLOTS * (c + 1)])

    def to_stage(c, value):
        for j in range(PAIRS):
            stage[2 * SLOTS * c : 2 * SLOTS * (c + 1), j * CHUNK : (j + 1) * CHUNK] = value[2 * SLOTS * j : 2 * SLOTS * (j + 1)]

    def remote(source, target, slot, sign, send, recv):
        return pltpu.make_async_remote_copy(
            src_ref=source.at[slot], dst_ref=target.at[slot], send_sem=send, recv_sem=recv,
            device_id=partner(slot, sign), device_id_type=MESH,
        )

    def send_some(source, target, q, start, stop, sign, send, recv):
        def one(i, carry):
            remote(source, target, q * SLOTS + i, sign, send, recv.at[q]).start()
            return carry

        lax.fori_loop(start, stop, one, 0)

    def keep_own(source, target):
        pltpu.make_async_copy(source.at[CHIPS - 1], target.at[CHIPS - 1], own_sem).start()

    def send_group(source, target, q, sign, send, recv):
        send_some(source, target, q, 0, SLOTS - lax.div(q, GROUPS - 1), sign, send, recv)

        @pl.when(q == GROUPS - 1)
        def _():
            keep_own(source, target)

    def wait_group(target, q, recv):
        @pl.when(q < GROUPS - 1)
        def _():
            ref = target.at[pl.ds(0, SLOTS)]
            pltpu.make_async_copy(ref, ref, recv.at[q]).wait()

        @pl.when(q == GROUPS - 1)
        def _():
            ref = target.at[pl.ds(0, SLOTS - 1)]
            pltpu.make_async_copy(ref, ref, recv.at[q]).wait()
            pltpu.make_async_copy(target.at[CHIPS - 1], target.at[CHIPS - 1], own_sem).wait()

    loads()[2].wait()

    def dispatch(t, carry):
        q = lax.rem(t + GROUPS - 1, GROUPS)
        for c in range(PIECES):
            value = jnp.dot(pick[q], tok[:, c * CHUNK : (c + 1) * CHUNK], preferred_element_type=F32)
            to_stage(c, value.astype(BF16))
        pack(sent, q)

        @pl.when(t == 0)
        def _():
            pl.semaphore_wait(barrier, CHIPS)

        start = jnp.where(t == 0, SLOTS - 1 - EARLY, 0)
        send_some(sent, got, q, start, jnp.where(t == 0, SLOTS - 1, SLOTS), 1, there_send, there_recv)
        return carry

    lax.fori_loop(0, GROUPS, dispatch, 0)
    send_some(sent, got, GROUPS - 1, 0, SLOTS - 1 - EARLY, 1, there_send, there_recv)
    keep_own(sent, got)
    for copy in loads()[3:]:
        copy.wait()

    def to_twin(source, target, send, recv):
        return pltpu.make_async_remote_copy(
            src_ref=source, dst_ref=target, send_sem=send, recv_sem=recv, device_id=twin, device_id_type=MESH
        )

    def over_rows(q):
        return to_twin(rows.at[q, pl.ds(0, OWN)], rows.at[q, pl.ds(OWN, OWN)], row_send.at[q], row_recv.at[q])

    def over_part(q, h):
        side = pl.ds(h * HALF, HALF)
        return to_twin(part_out.at[q, :, side], part_in.at[q, :, side], part_send.at[2 * q + h], part_recv.at[2 * q + h])

    def arrive(q):
        wait_group(got, q, there_recv)

        def put(r, c, value):
            rows[q, r, c] = value

        unpack(got, q, put)
        over_rows(q).start()

    arrive(0)

    def work(q, carry):
        over_rows(q).wait_recv()

        def up(t, carry):
            lane = pl.ds(pl.multiple_of(t * 256, 256), 256)
            gate = jnp.dot(rows[q], w_gate[:, lane], preferred_element_type=F32)
            upper = jnp.dot(rows[q], w_up[:, lane], preferred_element_type=F32)
            hidden[:, lane] = (gate / (1.0 + jnp.exp(-gate)) * upper).astype(BF16)
            return carry

        lax.fori_loop(0, 3, up, 0)

        for h in range(2):
            def down(t, carry):
                lane = pl.ds(pl.multiple_of(h * HALF + t * CHUNK, CHUNK), CHUNK)
                part = jnp.dot(hidden[...], w_down[:, lane], preferred_element_type=F32).astype(BF16)
                part_own[:, lane] = part[:OWN]
                part_out[q, :, lane] = part[OWN:]
                return carry

            lax.fori_loop(0, PIECES // 2, down, 0)
            over_part(q, h).start()

        @pl.when(q < GROUPS - 1)
        def _():
            arrive(q + 1)

        for c in range(PIECES):
            if c % (PIECES // 2) == 0:
                over_part(q, c // (PIECES // 2)).wait_recv()
            lane = slice(c * CHUNK, (c + 1) * CHUNK)
            to_stage(c, (part_own[:, lane].astype(F32) + part_in[q, :, lane].astype(F32)).astype(BF16))
        pack(answer, q)
        send_group(answer, back, q, -1, back_send, back_recv)
        return carry

    lax.fori_loop(0, GROUPS, work, 0)

    total[...] = jnp.zeros_like(total)

    def finish(q, carry):
        wait_group(back, q, back_recv)

        def put(r, c, value):
            flat[r, c] = value

        unpack(back, q, put)
        for c in range(PIECES):
            lane = slice(c * CHUNK, (c + 1) * CHUNK)
            for h in range(2):
                total[:, lane] += lax.dot_general(mixing[h, q], flat[:, lane], (((0,), (0,)), ((), ())), preferred_element_type=F32)
        return carry

    lax.fori_loop(0, GROUPS, finish, 0)
    out[...] = total[...].astype(BF16)
    for q in range(GROUPS):
        over_rows(q).wait_send()
        for h in range(2):
            over_part(q, h).wait_send()
    for source, send in ((sent, there_send), (answer, back_send)):
        ref = source.at[pl.ds(0, CHIPS - 1)]
        pltpu.make_async_copy(ref, ref, send).wait()


def body(tokens, expert_ids, gate_scores, w_gate, w_up, w_down):
    rows, width = tokens.shape
    half = w_gate.shape[2]
    blocks = (CHIPS, 2 * PIECES, LANES)
    m = 2 * SLOTS * PIECES
    vmem, hbm = pl.BlockSpec(memory_space=pltpu.VMEM), pl.BlockSpec(memory_space=pl.ANY)
    far = pl.BlockSpec(memory_space=pltpu.HBM)
    dma = pltpu.SemaphoreType.DMA
    return pl.pallas_call(
        kernel,
        out_shape=jax.ShapeDtypeStruct((rows, width), BF16),
        in_specs=[far, far, hbm, hbm, hbm, hbm],
        out_specs=vmem,
        scratch_shapes=[
            pltpu.VMEM(expert_ids.shape[::-1], jnp.int32),
            pltpu.VMEM(gate_scores.shape[::-1], F32),
            pltpu.VMEM((rows, width), BF16),
            pltpu.VMEM((width, half), BF16),
            pltpu.VMEM((width, half), BF16),
            pltpu.VMEM((half, width), BF16),
            pltpu.VMEM(blocks, BF16),
            pltpu.VMEM(blocks, BF16),
            pltpu.VMEM((GROUPS, 2 * OWN, width), BF16),
            pltpu.VMEM((2 * OWN, half), BF16),
            pltpu.VMEM((OWN, width), BF16),
            pltpu.VMEM((GROUPS, OWN, width), BF16),
            pltpu.VMEM((GROUPS, OWN, width), BF16),
            pltpu.VMEM(blocks, BF16),
            pltpu.VMEM(blocks, BF16),
            pltpu.VMEM((GROUPS, OWN, rows), BF16),
            pltpu.VMEM((2, GROUPS, OWN, rows), BF16),
            pltpu.VMEM((m, m), BF16),
            pltpu.VMEM((m, m), BF16),
            pltpu.VMEM((m, LANES), BF16),
            pltpu.VMEM((OWN, width), BF16),
            pltpu.VMEM((rows, width), F32),
            dma((6,)),
            dma, dma((GROUPS,)),
            dma((GROUPS,)), dma((GROUPS,)),
            dma((2 * GROUPS,)), dma((2 * GROUPS,)),
            dma, dma((GROUPS,)),
            dma,
        ],
        compiler_params=pltpu.CompilerParams(collective_id=0, has_side_effects=True, vmem_limit_bytes=52 << 20),
    )(expert_ids.T, gate_scores.T, tokens, w_gate, w_up, w_down)


def solution(mesh):
    split = ("group", "local")
    flat, deep = P(split, None), P(split, None, None)
    return jax.shard_map(
        body, mesh=mesh, in_specs=(flat, flat, flat, deep, deep, deep), out_specs=flat, check_vma=False
    )
```

```python
import jax
import jax.numpy as jnp
from jax import lax
from jax.experimental import pallas as pl
from jax.experimental.pallas import tpu as pltpu
from jax.sharding import PartitionSpec as P

MESH = pl.DeviceIdType.MESH
BF16, F32 = jnp.bfloat16, jnp.float32

SIDE = 4
CHIPS = SIDE**3
CAP = 6
GROUPS = 4
SLOTS = CHIPS // GROUPS
CHUNK = 512
PIECES = 8
PAIRS = CAP // 2
LANES = PAIRS * CHUNK
SIDES = 4
HALF = PIECES // SIDES * CHUNK
OWN = SLOTS * CAP
STRIDE = 13
EARLY = 1


def shift_of(slot):
    return 1 + lax.rem((slot + EARLY) * STRIDE, CHIPS - 1)


def kernel(
    ids_hbm, scores_hbm, tok_hbm, gate_hbm, up_hbm, down_hbm, out,
    ids, scores, tok, w_gate, w_up, w_down,
    sent, got, rows, hidden, part_own, part_out, part_in, answer, back,
    pick, mixing, spread, unspread, stage, flat, total,
    load_sem, there_send, there_recv, row_send, row_recv, part_send, part_recv, back_send, back_recv, own_sem,
):
    group, local = lax.axis_index("group"), lax.axis_index("local")
    x, z = lax.div(group, SIDE), lax.rem(group, SIDE)
    y, core = lax.div(local, 2), lax.rem(local, 2)
    twin = (group, local + 1 - 2 * core)

    def partner(slot, sign):
        shift = shift_of(slot)
        far_x = lax.rem(x + SIDE + sign * lax.div(shift, SIDE * SIDE), SIDE)
        far_y = lax.rem(y + SIDE + sign * lax.rem(lax.div(shift, SIDE), SIDE), SIDE)
        far_z = lax.rem(z + SIDE + sign * lax.rem(shift, SIDE), SIDE)
        return (far_x * SIDE + far_z, far_y * 2 + core)

    def loads():
        pairs = (
            (ids_hbm, ids), (scores_hbm, scores), (tok_hbm, tok),
            (gate_hbm.at[0], w_gate), (up_hbm.at[0], w_up), (down_hbm.at[0], w_down),
        )
        return [pltpu.make_async_copy(a, b, load_sem.at[n]) for n, (a, b) in enumerate(pairs)]

    barrier = pltpu.get_barrier_semaphore()

    for copy in loads()[:3]:
        copy.start()
    along = [[lax.rem(v + d, SIDE) for d in range(SIDE)] for v in (x, y, z)]
    for dx in (2, 1, 3, 0):
        for dz in (2, 1, 3, 0):
            wide = along[0][dx] * SIDE + along[2][dz]
            for dy in (2, 1, 3, 0):
                if dx or dy or dz:
                    pl.semaphore_signal(barrier, inc=1, device_id=(wide, along[1][dy] * 2 + core), device_id_type=MESH)
    pl.semaphore_signal(barrier, inc=1, device_id=twin, device_id_type=MESH)
    for copy in loads()[:2]:
        copy.wait()

    n = 2 * CHIPS
    row = lax.broadcasted_iota(jnp.int32, (n, n), 0)
    column = lax.broadcasted_iota(jnp.int32, (n, n), 1)
    slot, odd = lax.shift_right_logical(row, 1), row & 1
    shift = jnp.where(slot == CHIPS - 1, 0, shift_of(slot))
    expert = ((x + lax.shift_right_logical(shift, 4)) & 3) * 16 + ((z + shift) & 3) * 4 + ((y + lax.shift_right_logical(shift, 2)) & 3)
    first, second = expert == ids[0:1, :], expert == ids[1:2, :]
    chosen = jnp.where(first | second, 1.0, 0.0)
    earlier = jnp.where(row < column, 1.0, 0.0).astype(BF16)
    rank = jnp.dot(chosen.astype(BF16), earlier, preferred_element_type=F32)
    scale = scores[0:1, :] + scores[1:2, :]
    weight = jnp.where(first, scores[0:1, :] / scale, 0.0) + jnp.where(second, scores[1:2, :] / scale, 0.0)
    for j in range(PAIRS):
        here = jnp.where(rank == (2 * j + odd).astype(F32), chosen, 0.0)
        high = (here * weight).astype(BF16)
        low = (here * weight - high.astype(F32)).astype(BF16)
        for q in range(GROUPS):
            part = slice(2 * SLOTS * q, 2 * SLOTS * (q + 1))
            place = slice(2 * SLOTS * j, 2 * SLOTS * (j + 1))
            pick[q, place, :] = here[part].astype(BF16)
            mixing[0, q, place, :] = high[part]
            mixing[1, q, place, :] = low[part]

    m = 2 * SLOTS * PIECES
    a = lax.broadcasted_iota(jnp.int32, (m, m), 0)
    b = lax.broadcasted_iota(jnp.int32, (m, m), 1)

    def meets(a, b):
        same = (lax.shift_right_logical(a, 4) == (lax.shift_right_logical(b, 1) & 15)) & ((lax.shift_right_logical(a, 1) & 7) == lax.shift_right_logical(b, 5)) & ((a & 1) == (b & 1))
        return jnp.where(same, 1.0, 0.0).astype(BF16)

    spread[...] = meets(a, b)
    unspread[...] = meets(b, a)

    def pack(target, q):
        for j in range(PAIRS):
            lane = slice(j * CHUNK, (j + 1) * CHUNK)
            block = jnp.dot(spread[...], stage[:, lane], preferred_element_type=F32).astype(BF16)
            target[pl.ds(q * SLOTS, SLOTS), :, lane] = block.reshape(SLOTS, 2 * PIECES, CHUNK)

    def unpack(source, q, put):
        for j in range(PAIRS):
            lane = slice(j * CHUNK, (j + 1) * CHUNK)
            block = source[pl.ds(q * SLOTS, SLOTS), :, lane].reshape(m, CHUNK)
            block = jnp.dot(unspread[...], block, preferred_element_type=F32).astype(BF16)
            for c in range(PIECES):
                put(slice(2 * SLOTS * j, 2 * SLOTS * (j + 1)), slice(c * CHUNK, (c + 1) * CHUNK), block[2 * SLOTS * c : 2 * SLOTS * (c + 1)])

    def to_stage(c, value):
        for j in range(PAIRS):
            stage[2 * SLOTS * c : 2 * SLOTS * (c + 1), j * CHUNK : (j + 1) * CHUNK] = value[2 * SLOTS * j : 2 * SLOTS * (j + 1)]

    def remote(source, target, slot, sign, send, recv):
        return pltpu.make_async_remote_copy(
            src_ref=source.at[slot], dst_ref=target.at[slot], send_sem=send, recv_sem=recv,
            device_id=partner(slot, sign), device_id_type=MESH,
        )

    def send_some(source, target, q, start, stop, sign, send, recv):
        def one(i, carry):
            remote(source, target, q * SLOTS + i, sign, send, recv.at[q]).start()
            return carry

        lax.fori_loop(start, stop, one, 0)

    def keep_own(source, target):
        pltpu.make_async_copy(source.at[CHIPS - 1], target.at[CHIPS - 1], own_sem).start()

    def send_group(source, target, q, sign, send, recv):
        send_some(source, target, q, 0, SLOTS - lax.div(q, GROUPS - 1), sign, send, recv)

        @pl.when(q == GROUPS - 1)
        def _():
            keep_own(source, target)

    def wait_group(target, q, recv):
        @pl.when(q < GROUPS - 1)
        def _():
            ref = target.at[pl.ds(0, SLOTS)]
            pltpu.make_async_copy(ref, ref, recv.at[q]).wait()

        @pl.when(q == GROUPS - 1)
        def _():
            ref = target.at[pl.ds(0, SLOTS - 1)]
            pltpu.make_async_copy(ref, ref, recv.at[q]).wait()
            pltpu.make_async_copy(target.at[CHIPS - 1], target.at[CHIPS - 1], own_sem).wait()

    loads()[2].wait()

    def dispatch(t, carry):
        q = lax.rem(t + GROUPS - 1, GROUPS)
        for c in range(PIECES):
            value = jnp.dot(pick[q], tok[:, c * CHUNK : (c + 1) * CHUNK], preferred_element_type=F32)
            to_stage(c, value.astype(BF16))
        pack(sent, q)

        @pl.when(t == 0)
        def _():
            pl.semaphore_wait(barrier, CHIPS)

        start = jnp.where(t == 0, SLOTS - 1 - EARLY, 0)
        send_some(sent, got, q, start, jnp.where(t == 0, SLOTS - 1, SLOTS), 1, there_send, there_recv)
        return carry

    lax.fori_loop(0, GROUPS, dispatch, 0)
    for copy in loads()[3:]:
        copy.start()
    send_some(sent, got, GROUPS - 1, 0, SLOTS - 1 - EARLY, 1, there_send, there_recv)
    keep_own(sent, got)
    for copy in loads()[3:]:
        copy.wait()

    def to_twin(source, target, send, recv):
        return pltpu.make_async_remote_copy(
            src_ref=source, dst_ref=target, send_sem=send, recv_sem=recv, device_id=twin, device_id_type=MESH
        )

    def over_rows(q):
        return to_twin(rows.at[q, pl.ds(0, OWN)], rows.at[q, pl.ds(OWN, OWN)], row_send.at[q], row_recv.at[q])

    def over_part(q, h):
        side = pl.ds(pl.multiple_of(h * HALF, HALF), HALF)
        return to_twin(part_out.at[q, :, side], part_in.at[q, :, side], part_send.at[SIDES * q + h], part_recv.at[SIDES * q + h])

    def arrive(q):
        wait_group(got, q, there_recv)

        def put(r, c, value):
            rows[q, r, c] = value

        unpack(got, q, put)
        over_rows(q).start()

    arrive(0)

    def work(q, carry):
        over_rows(q).wait_recv()

        def up(t, carry):
            lane = pl.ds(pl.multiple_of(t * 256, 256), 256)
            gate = jnp.dot(rows[q], w_gate[:, lane], preferred_element_type=F32)
            upper = jnp.dot(rows[q], w_up[:, lane], preferred_element_type=F32)
            hidden[:, lane] = (gate / (1.0 + jnp.exp(-gate)) * upper).astype(BF16)
            return carry

        lax.fori_loop(0, 3, up, 0)

        def side(h, carry):
            def down(t, carry):
                lane = pl.ds(pl.multiple_of(h * HALF + t * CHUNK, CHUNK), CHUNK)
                part = jnp.dot(hidden[...], w_down[:, lane], preferred_element_type=F32).astype(BF16)
                part_own[:, lane] = part[:OWN]
                part_out[q, :, lane] = part[OWN:]
                return carry

            lax.fori_loop(0, PIECES // SIDES, down, 0)
            over_part(q, h).start()
            return carry

        lax.fori_loop(0, SIDES, side, 0)

        @pl.when(q < GROUPS - 1)
        def _():
            arrive(q + 1)

        for c in range(PIECES):
            if c % (PIECES // SIDES) == 0:
                over_part(q, c // (PIECES // SIDES)).wait_recv()
            lane = slice(c * CHUNK, (c + 1) * CHUNK)
            to_stage(c, (part_own[:, lane].astype(F32) + part_in[q, :, lane].astype(F32)).astype(BF16))
        pack(answer, q)
        send_group(answer, back, q, -1, back_send, back_recv)
        return carry

    lax.fori_loop(0, GROUPS, work, 0)

    total[...] = jnp.zeros_like(total)

    def finish(q, put_sum):
        wait_group(back, q, back_recv)

        def put(r, c, value):
            flat[r, c] = value

        unpack(back, q, put)
        for c in range(PIECES):
            lane = slice(c * CHUNK, (c + 1) * CHUNK)
            high, low = (
                lax.dot_general(mixing[h, q], flat[:, lane], (((0,), (0,)), ((), ())), preferred_element_type=F32)
                for h in range(2)
            )
            put_sum(lane, total[:, lane] + high + low)

    def keep(lane, value):
        total[:, lane] = value

    def leave(lane, value):
        out[:, lane] = value.astype(BF16)

    def early(q, carry):
        finish(q, keep)
        return carry

    lax.fori_loop(0, GROUPS - 1, early, 0)
    finish(GROUPS - 1, leave)
    for q in range(GROUPS):
        over_rows(q).wait_send()
        for h in range(SIDES):
            over_part(q, h).wait_send()
    for source, send in ((sent, there_send), (answer, back_send)):
        ref = source.at[pl.ds(0, CHIPS - 1)]
        pltpu.make_async_copy(ref, ref, send).wait()


def body(tokens, expert_ids, gate_scores, w_gate, w_up, w_down):
    rows, width = tokens.shape
    half = w_gate.shape[2]
    blocks = (CHIPS, 2 * PIECES, LANES)
    m = 2 * SLOTS * PIECES
    vmem, hbm = pl.BlockSpec(memory_space=pltpu.VMEM), pl.BlockSpec(memory_space=pl.ANY)
    far = pl.BlockSpec(memory_space=pltpu.HBM)
    dma = pltpu.SemaphoreType.DMA
    return pl.pallas_call(
        kernel,
        out_shape=jax.ShapeDtypeStruct((rows, width), BF16),
        in_specs=[far, far, hbm, hbm, hbm, hbm],
        out_specs=vmem,
        scratch_shapes=[
            pltpu.VMEM(expert_ids.shape[::-1], jnp.int32),
            pltpu.VMEM(gate_scores.shape[::-1], F32),
            pltpu.VMEM((rows, width), BF16),
            pltpu.VMEM((width, half), BF16),
            pltpu.VMEM((width, half), BF16),
            pltpu.VMEM((half, width), BF16),
            pltpu.VMEM(blocks, BF16),
            pltpu.VMEM(blocks, BF16),
            pltpu.VMEM((GROUPS, 2 * OWN, width), BF16),
            pltpu.VMEM((2 * OWN, half), BF16),
            pltpu.VMEM((OWN, width), BF16),
            pltpu.VMEM((GROUPS, OWN, width), BF16),
            pltpu.VMEM((GROUPS, OWN, width), BF16),
            pltpu.VMEM(blocks, BF16),
            pltpu.VMEM(blocks, BF16),
            pltpu.VMEM((GROUPS, OWN, rows), BF16),
            pltpu.VMEM((2, GROUPS, OWN, rows), BF16),
            pltpu.VMEM((m, m), BF16),
            pltpu.VMEM((m, m), BF16),
            pltpu.VMEM((m, LANES), BF16),
            pltpu.VMEM((OWN, width), BF16),
            pltpu.VMEM((rows, width), F32),
            dma((6,)),
            dma, dma((GROUPS,)),
            dma((GROUPS,)), dma((GROUPS,)),
            dma((SIDES * GROUPS,)), dma((SIDES * GROUPS,)),
            dma, dma((GROUPS,)),
            dma,
        ],
        compiler_params=pltpu.CompilerParams(collective_id=0, has_side_effects=True, vmem_limit_bytes=52 << 20),
    )(expert_ids.T, gate_scores.T, tokens, w_gate, w_up, w_down)


def solution(mesh):
    split = ("group", "local")
    flat, deep = P(split, None), P(split, None, None)
    return jax.shard_map(
        body, mesh=mesh, in_specs=(flat, flat, flat, deep, deep, deep), out_specs=flat, check_vma=False
    )
```

```python
import jax
import jax.numpy as jnp
from jax import lax
from jax.experimental import pallas as pl
from jax.experimental.pallas import tpu as pltpu
from jax.sharding import PartitionSpec as P

MESH = pl.DeviceIdType.MESH
BF16, F32 = jnp.bfloat16, jnp.float32

SIDE = 4
CHIPS = SIDE**3
CAP = 6
GROUPS = 4
SLOTS = CHIPS // GROUPS
CHUNK = 512
PIECES = 8
PAIRS = CAP // 2
LANES = PAIRS * CHUNK
SIDES = 4
HALF = PIECES // SIDES * CHUNK
OWN = SLOTS * CAP
STRIDE = 13
APART = 31
EARLY = 1


def shift_of(slot, core):
    return 1 + lax.rem((slot + EARLY + core * APART) * STRIDE, CHIPS - 1)


def kernel(
    ids_hbm, scores_hbm, tok_hbm, gate_hbm, up_hbm, down_hbm, out,
    ids, scores, tok, w_gate, w_up, w_down,
    sent, got, rows, hidden, part_own, part_out, part_in, answer, back,
    pick, mixing, spread, unspread, stage, flat, total,
    load_sem, there_send, there_recv, row_send, row_recv, part_send, part_recv, back_send, back_recv, own_sem,
):
    group, local = lax.axis_index("group"), lax.axis_index("local")
    x, z = lax.div(group, SIDE), lax.rem(group, SIDE)
    y, core = lax.div(local, 2), lax.rem(local, 2)
    twin = (group, local + 1 - 2 * core)

    def partner(slot, sign):
        shift = shift_of(slot, core)
        far_x = lax.rem(x + SIDE + sign * lax.div(shift, SIDE * SIDE), SIDE)
        far_y = lax.rem(y + SIDE + sign * lax.rem(lax.div(shift, SIDE), SIDE), SIDE)
        far_z = lax.rem(z + SIDE + sign * lax.rem(shift, SIDE), SIDE)
        return (far_x * SIDE + far_z, far_y * 2 + core)

    def loads():
        pairs = (
            (ids_hbm, ids), (scores_hbm, scores), (tok_hbm, tok),
            (gate_hbm.at[0], w_gate), (up_hbm.at[0], w_up), (down_hbm.at[0], w_down),
        )
        return [pltpu.make_async_copy(a, b, load_sem.at[n]) for n, (a, b) in enumerate(pairs)]

    barrier = pltpu.get_barrier_semaphore()

    for copy in loads()[:3]:
        copy.start()
    along = [[lax.rem(v + d, SIDE) for d in range(SIDE)] for v in (x, y, z)]
    for dx in (2, 1, 3, 0):
        for dz in (2, 1, 3, 0):
            wide = along[0][dx] * SIDE + along[2][dz]
            for dy in (2, 1, 3, 0):
                if dx or dy or dz:
                    pl.semaphore_signal(barrier, inc=1, device_id=(wide, along[1][dy] * 2 + core), device_id_type=MESH)
    pl.semaphore_signal(barrier, inc=1, device_id=twin, device_id_type=MESH)
    for copy in loads()[:2]:
        copy.wait()

    n = 2 * CHIPS
    row = lax.broadcasted_iota(jnp.int32, (n, n), 0)
    column = lax.broadcasted_iota(jnp.int32, (n, n), 1)
    slot, odd = lax.shift_right_logical(row, 1), row & 1
    shift = jnp.where(slot == CHIPS - 1, 0, shift_of(slot, core))
    expert = ((x + lax.shift_right_logical(shift, 4)) & 3) * 16 + ((z + shift) & 3) * 4 + ((y + lax.shift_right_logical(shift, 2)) & 3)
    first, second = expert == ids[0:1, :], expert == ids[1:2, :]
    chosen = jnp.where(first | second, 1.0, 0.0)
    earlier = jnp.where(row < column, 1.0, 0.0).astype(BF16)
    rank = jnp.dot(chosen.astype(BF16), earlier, preferred_element_type=F32)
    scale = scores[0:1, :] + scores[1:2, :]
    weight = jnp.where(first, scores[0:1, :] / scale, 0.0) + jnp.where(second, scores[1:2, :] / scale, 0.0)
    for j in range(PAIRS):
        here = jnp.where(rank == (2 * j + odd).astype(F32), chosen, 0.0)
        high = (here * weight).astype(BF16)
        low = (here * weight - high.astype(F32)).astype(BF16)
        for q in range(GROUPS):
            part = slice(2 * SLOTS * q, 2 * SLOTS * (q + 1))
            place = slice(2 * SLOTS * j, 2 * SLOTS * (j + 1))
            pick[q, place, :] = here[part].astype(BF16)
            mixing[0, q, place, :] = high[part]
            mixing[1, q, place, :] = low[part]

    m = 2 * SLOTS * PIECES
    a = lax.broadcasted_iota(jnp.int32, (m, m), 0)
    b = lax.broadcasted_iota(jnp.int32, (m, m), 1)

    def meets(a, b):
        same = (lax.shift_right_logical(a, 4) == (lax.shift_right_logical(b, 1) & 15)) & ((lax.shift_right_logical(a, 1) & 7) == lax.shift_right_logical(b, 5)) & ((a & 1) == (b & 1))
        return jnp.where(same, 1.0, 0.0).astype(BF16)

    spread[...] = meets(a, b)
    unspread[...] = meets(b, a)

    def pack(target, q):
        for j in range(PAIRS):
            lane = slice(j * CHUNK, (j + 1) * CHUNK)
            block = jnp.dot(spread[...], stage[:, lane], preferred_element_type=F32).astype(BF16)
            target[pl.ds(q * SLOTS, SLOTS), :, lane] = block.reshape(SLOTS, 2 * PIECES, CHUNK)

    def unpack(source, q, put):
        for j in range(PAIRS):
            lane = slice(j * CHUNK, (j + 1) * CHUNK)
            block = source[pl.ds(q * SLOTS, SLOTS), :, lane].reshape(m, CHUNK)
            block = jnp.dot(unspread[...], block, preferred_element_type=F32).astype(BF16)
            for c in range(PIECES):
                put(slice(2 * SLOTS * j, 2 * SLOTS * (j + 1)), slice(c * CHUNK, (c + 1) * CHUNK), block[2 * SLOTS * c : 2 * SLOTS * (c + 1)])

    def to_stage(c, value):
        for j in range(PAIRS):
            stage[2 * SLOTS * c : 2 * SLOTS * (c + 1), j * CHUNK : (j + 1) * CHUNK] = value[2 * SLOTS * j : 2 * SLOTS * (j + 1)]

    def remote(source, target, slot, sign, send, recv):
        return pltpu.make_async_remote_copy(
            src_ref=source.at[slot], dst_ref=target.at[slot], send_sem=send, recv_sem=recv,
            device_id=partner(slot, sign), device_id_type=MESH,
        )

    def send_some(source, target, q, start, stop, sign, send, recv):
        def one(i, carry):
            remote(source, target, q * SLOTS + i, sign, send, recv.at[q]).start()
            return carry

        lax.fori_loop(start, stop, one, 0)

    def keep_own(source, target):
        pltpu.make_async_copy(source.at[CHIPS - 1], target.at[CHIPS - 1], own_sem).start()

    def send_group(source, target, q, sign, send, recv):
        send_some(source, target, q, 0, SLOTS - lax.div(q, GROUPS - 1), sign, send, recv)

        @pl.when(q == GROUPS - 1)
        def _():
            keep_own(source, target)

    def wait_group(target, q, recv):
        @pl.when(q < GROUPS - 1)
        def _():
            ref = target.at[pl.ds(0, SLOTS)]
            pltpu.make_async_copy(ref, ref, recv.at[q]).wait()

        @pl.when(q == GROUPS - 1)
        def _():
            ref = target.at[pl.ds(0, SLOTS - 1)]
            pltpu.make_async_copy(ref, ref, recv.at[q]).wait()
            pltpu.make_async_copy(target.at[CHIPS - 1], target.at[CHIPS - 1], own_sem).wait()

    loads()[2].wait()

    def dispatch(t, carry):
        q = lax.rem(t + GROUPS - 1, GROUPS)
        for c in range(PIECES):
            value = jnp.dot(pick[q], tok[:, c * CHUNK : (c + 1) * CHUNK], preferred_element_type=F32)
            to_stage(c, value.astype(BF16))
        pack(sent, q)

        @pl.when(t == 0)
        def _():
            pl.semaphore_wait(barrier, CHIPS)

        start = jnp.where(t == 0, SLOTS - 1 - EARLY, 0)
        send_some(sent, got, q, start, jnp.where(t == 0, SLOTS - 1, SLOTS), 1, there_send, there_recv)
        return carry

    lax.fori_loop(0, GROUPS, dispatch, 0)
    for copy in loads()[3:]:
        copy.start()
    send_some(sent, got, GROUPS - 1, 0, SLOTS - 1 - EARLY, 1, there_send, there_recv)
    keep_own(sent, got)
    for copy in loads()[3:]:
        copy.wait()

    def to_twin(source, target, send, recv):
        return pltpu.make_async_remote_copy(
            src_ref=source, dst_ref=target, send_sem=send, recv_sem=recv, device_id=twin, device_id_type=MESH
        )

    def over_rows(q):
        return to_twin(rows.at[q, pl.ds(0, OWN)], rows.at[q, pl.ds(OWN, OWN)], row_send.at[q], row_recv.at[q])

    def over_part(q, h):
        side = pl.ds(pl.multiple_of(h * HALF, HALF), HALF)
        return to_twin(part_out.at[q, :, side], part_in.at[q, :, side], part_send.at[SIDES * q + h], part_recv.at[SIDES * q + h])

    def arrive(q):
        wait_group(got, q, there_recv)

        def put(r, c, value):
            rows[q, r, c] = value

        unpack(got, q, put)
        over_rows(q).start()

    arrive(0)

    def work(q, carry):
        over_rows(q).wait_recv()

        def up(t, carry):
            lane = pl.ds(pl.multiple_of(t * 256, 256), 256)
            gate = jnp.dot(rows[q], w_gate[:, lane], preferred_element_type=F32)
            upper = jnp.dot(rows[q], w_up[:, lane], preferred_element_type=F32)
            hidden[:, lane] = (gate / (1.0 + jnp.exp(-gate)) * upper).astype(BF16)
            return carry

        lax.fori_loop(0, 3, up, 0)

        def side(h, carry):
            def down(t, carry):
                lane = pl.ds(pl.multiple_of(h * HALF + t * CHUNK, CHUNK), CHUNK)
                part = jnp.dot(hidden[...], w_down[:, lane], preferred_element_type=F32).astype(BF16)
                part_own[:, lane] = part[:OWN]
                part_out[q, :, lane] = part[OWN:]
                return carry

            lax.fori_loop(0, PIECES // SIDES, down, 0)
            over_part(q, h).start()
            return carry

        lax.fori_loop(0, SIDES, side, 0)

        @pl.when(q < GROUPS - 1)
        def _():
            arrive(q + 1)

        for c in range(PIECES):
            if c % (PIECES // SIDES) == 0:
                over_part(q, c // (PIECES // SIDES)).wait_recv()
            lane = slice(c * CHUNK, (c + 1) * CHUNK)
            to_stage(c, (part_own[:, lane].astype(F32) + part_in[q, :, lane].astype(F32)).astype(BF16))
        pack(answer, q)
        send_group(answer, back, q, -1, back_send, back_recv)
        return carry

    lax.fori_loop(0, GROUPS, work, 0)

    total[...] = jnp.zeros_like(total)

    def finish(q, put_sum):
        wait_group(back, q, back_recv)

        def put(r, c, value):
            flat[r, c] = value

        unpack(back, q, put)
        for c in range(PIECES):
            lane = slice(c * CHUNK, (c + 1) * CHUNK)
            high, low = (
                lax.dot_general(mixing[h, q], flat[:, lane], (((0,), (0,)), ((), ())), preferred_element_type=F32)
                for h in range(2)
            )
            put_sum(lane, total[:, lane] + high + low)

    def keep(lane, value):
        total[:, lane] = value

    def leave(lane, value):
        out[:, lane] = value.astype(BF16)

    def early(q, carry):
        finish(q, keep)
        return carry

    lax.fori_loop(0, GROUPS - 1, early, 0)
    finish(GROUPS - 1, leave)
    for q in range(GROUPS):
        over_rows(q).wait_send()
        for h in range(SIDES):
            over_part(q, h).wait_send()
    for source, send in ((sent, there_send), (answer, back_send)):
        ref = source.at[pl.ds(0, CHIPS - 1)]
        pltpu.make_async_copy(ref, ref, send).wait()


def body(tokens, expert_ids, gate_scores, w_gate, w_up, w_down):
    rows, width = tokens.shape
    half = w_gate.shape[2]
    blocks = (CHIPS, 2 * PIECES, LANES)
    m = 2 * SLOTS * PIECES
    vmem, hbm = pl.BlockSpec(memory_space=pltpu.VMEM), pl.BlockSpec(memory_space=pl.ANY)
    far = pl.BlockSpec(memory_space=pltpu.HBM)
    dma = pltpu.SemaphoreType.DMA
    return pl.pallas_call(
        kernel,
        out_shape=jax.ShapeDtypeStruct((rows, width), BF16),
        in_specs=[far, far, hbm, hbm, hbm, hbm],
        out_specs=vmem,
        scratch_shapes=[
            pltpu.VMEM(expert_ids.shape[::-1], jnp.int32),
            pltpu.VMEM(gate_scores.shape[::-1], F32),
            pltpu.VMEM((rows, width), BF16),
            pltpu.VMEM((width, half), BF16),
            pltpu.VMEM((width, half), BF16),
            pltpu.VMEM((half, width), BF16),
            pltpu.VMEM(blocks, BF16),
            pltpu.VMEM(blocks, BF16),
            pltpu.VMEM((GROUPS, 2 * OWN, width), BF16),
            pltpu.VMEM((2 * OWN, half), BF16),
            pltpu.VMEM((OWN, width), BF16),
            pltpu.VMEM((GROUPS, OWN, width), BF16),
            pltpu.VMEM((GROUPS, OWN, width), BF16),
            pltpu.VMEM(blocks, BF16),
            pltpu.VMEM(blocks, BF16),
            pltpu.VMEM((GROUPS, OWN, rows), BF16),
            pltpu.VMEM((2, GROUPS, OWN, rows), BF16),
            pltpu.VMEM((m, m), BF16),
            pltpu.VMEM((m, m), BF16),
            pltpu.VMEM((m, LANES), BF16),
            pltpu.VMEM((OWN, width), BF16),
            pltpu.VMEM((rows, width), F32),
            dma((6,)),
            dma, dma((GROUPS,)),
            dma((GROUPS,)), dma((GROUPS,)),
            dma((SIDES * GROUPS,)), dma((SIDES * GROUPS,)),
            dma, dma((GROUPS,)),
            dma,
        ],
        compiler_params=pltpu.CompilerParams(collective_id=0, has_side_effects=True, vmem_limit_bytes=52 << 20),
    )(expert_ids.T, gate_scores.T, tokens, w_gate, w_up, w_down)


def solution(mesh):
    split = ("group", "local")
    flat, deep = P(split, None), P(split, None, None)
    return jax.shard_map(
        body, mesh=mesh, in_specs=(flat, flat, flat, deep, deep, deep), out_specs=flat, check_vma=False
    )
```

```python
import jax
import jax.numpy as jnp
from jax import lax
from jax.experimental import pallas as pl
from jax.experimental.pallas import tpu as pltpu
from jax.sharding import PartitionSpec as P

MESH = pl.DeviceIdType.MESH
BF16, F32 = jnp.bfloat16, jnp.float32

SIDE = 4
CHIPS = SIDE**3
CAP = 6
GROUPS = 4
SLOTS = CHIPS // GROUPS
CHUNK = 512
PIECES = 8
PAIRS = CAP // 2
LANES = PAIRS * CHUNK
SIDES = 4
HALF = PIECES // SIDES * CHUNK
OWN = SLOTS * CAP
STRIDE = 13
EARLY = 1


def shift_of(slot):
    return 1 + lax.rem((slot + EARLY) * STRIDE, CHIPS - 1)


def kernel(
    ids_hbm, scores_hbm, tok_hbm, gate_hbm, up_hbm, down_hbm, out,
    ids, scores, tok, w_gate, w_up, w_down,
    sent, got, rows, hidden, part_own, part_out, part_in, answer, back,
    pick, mixing, spread, unspread, stage, flat, total,
    load_sem, there_send, there_recv, row_send, row_recv, part_send, part_recv, back_send, back_recv, own_sem,
):
    group, local = lax.axis_index("group"), lax.axis_index("local")
    x, z = lax.div(group, SIDE), lax.rem(group, SIDE)
    y, core = lax.div(local, 2), lax.rem(local, 2)
    twin = (group, local + 1 - 2 * core)

    def partner(slot, sign):
        shift = shift_of(slot)
        far_x = lax.rem(x + SIDE + sign * lax.div(shift, SIDE * SIDE), SIDE)
        far_y = lax.rem(y + SIDE + sign * lax.rem(lax.div(shift, SIDE), SIDE), SIDE)
        far_z = lax.rem(z + SIDE + sign * lax.rem(shift, SIDE), SIDE)
        return (far_x * SIDE + far_z, far_y * 2 + core)

    def loads():
        pairs = (
            (ids_hbm, ids), (scores_hbm, scores), (tok_hbm, tok),
            (gate_hbm.at[0], w_gate), (up_hbm.at[0], w_up), (down_hbm.at[0], w_down),
        )
        return [pltpu.make_async_copy(a, b, load_sem.at[n]) for n, (a, b) in enumerate(pairs)]

    barrier = pltpu.get_barrier_semaphore()

    along = [[lax.rem(v + d, SIDE) for d in range(SIDE)] for v in (x, y, z)]
    for dx in (2, 1, 3, 0):
        for dz in (2, 1, 3, 0):
            wide = along[0][dx] * SIDE + along[2][dz]
            for dy in (2, 1, 3, 0):
                if dx or dy or dz:
                    pl.semaphore_signal(barrier, inc=1, device_id=(wide, along[1][dy] * 2 + core), device_id_type=MESH)
    pl.semaphore_signal(barrier, inc=1, device_id=twin, device_id_type=MESH)
    for copy in loads()[:3]:
        copy.start()
    for copy in loads()[:2]:
        copy.wait()

    n = 2 * CHIPS
    row = lax.broadcasted_iota(jnp.int32, (n, n), 0)
    column = lax.broadcasted_iota(jnp.int32, (n, n), 1)
    slot, odd = lax.shift_right_logical(row, 1), row & 1
    shift = jnp.where(slot == CHIPS - 1, 0, shift_of(slot))
    expert = ((x + lax.shift_right_logical(shift, 4)) & 3) * 16 + ((z + shift) & 3) * 4 + ((y + lax.shift_right_logical(shift, 2)) & 3)
    first, second = expert == ids[0:1, :], expert == ids[1:2, :]
    chosen = jnp.where(first | second, 1.0, 0.0)
    earlier = jnp.where(row < column, 1.0, 0.0).astype(BF16)
    rank = jnp.dot(chosen.astype(BF16), earlier, preferred_element_type=F32)
    scale = scores[0:1, :] + scores[1:2, :]
    weight = jnp.where(first, scores[0:1, :] / scale, 0.0) + jnp.where(second, scores[1:2, :] / scale, 0.0)
    for j in range(PAIRS):
        here = jnp.where(rank == (2 * j + odd).astype(F32), chosen, 0.0)
        high = (here * weight).astype(BF16)
        low = (here * weight - high.astype(F32)).astype(BF16)
        for q in range(GROUPS):
            part = slice(2 * SLOTS * q, 2 * SLOTS * (q + 1))
            place = slice(2 * SLOTS * j, 2 * SLOTS * (j + 1))
            pick[q, place, :] = here[part].astype(BF16)
            mixing[0, q, place, :] = high[part]
            mixing[1, q, place, :] = low[part]

    m = 2 * SLOTS * PIECES
    a = lax.broadcasted_iota(jnp.int32, (m, m), 0)
    b = lax.broadcasted_iota(jnp.int32, (m, m), 1)

    def meets(a, b):
        same = (lax.shift_right_logical(a, 4) == (lax.shift_right_logical(b, 1) & 15)) & ((lax.shift_right_logical(a, 1) & 7) == lax.shift_right_logical(b, 5)) & ((a & 1) == (b & 1))
        return jnp.where(same, 1.0, 0.0).astype(BF16)

    spread[...] = meets(a, b)
    unspread[...] = meets(b, a)

    def pack(target, q):
        for j in range(PAIRS):
            lane = slice(j * CHUNK, (j + 1) * CHUNK)
            block = jnp.dot(spread[...], stage[:, lane], preferred_element_type=F32).astype(BF16)
            target[pl.ds(q * SLOTS, SLOTS), :, lane] = block.reshape(SLOTS, 2 * PIECES, CHUNK)

    def unpack(source, q, put):
        for j in range(PAIRS):
            lane = slice(j * CHUNK, (j + 1) * CHUNK)
            block = source[pl.ds(q * SLOTS, SLOTS), :, lane].reshape(m, CHUNK)
            block = jnp.dot(unspread[...], block, preferred_element_type=F32).astype(BF16)
            for c in range(PIECES):
                put(slice(2 * SLOTS * j, 2 * SLOTS * (j + 1)), slice(c * CHUNK, (c + 1) * CHUNK), block[2 * SLOTS * c : 2 * SLOTS * (c + 1)])

    def to_stage(c, value):
        for j in range(PAIRS):
            stage[2 * SLOTS * c : 2 * SLOTS * (c + 1), j * CHUNK : (j + 1) * CHUNK] = value[2 * SLOTS * j : 2 * SLOTS * (j + 1)]

    def remote(source, target, slot, sign, send, recv):
        return pltpu.make_async_remote_copy(
            src_ref=source.at[slot], dst_ref=target.at[slot], send_sem=send, recv_sem=recv,
            device_id=partner(slot, sign), device_id_type=MESH,
        )

    def send_some(source, target, q, start, stop, sign, send, recv):
        def one(i, carry):
            remote(source, target, q * SLOTS + i, sign, send, recv.at[q]).start()
            return carry

        lax.fori_loop(start, stop, one, 0)

    def keep_own(source, target):
        pltpu.make_async_copy(source.at[CHIPS - 1], target.at[CHIPS - 1], own_sem).start()

    def send_group(source, target, q, sign, send, recv):
        send_some(source, target, q, 0, SLOTS - lax.div(q, GROUPS - 1), sign, send, recv)

        @pl.when(q == GROUPS - 1)
        def _():
            keep_own(source, target)

    def wait_group(target, q, recv):
        @pl.when(q < GROUPS - 1)
        def _():
            ref = target.at[pl.ds(0, SLOTS)]
            pltpu.make_async_copy(ref, ref, recv.at[q]).wait()

        @pl.when(q == GROUPS - 1)
        def _():
            ref = target.at[pl.ds(0, SLOTS - 1)]
            pltpu.make_async_copy(ref, ref, recv.at[q]).wait()
            pltpu.make_async_copy(target.at[CHIPS - 1], target.at[CHIPS - 1], own_sem).wait()

    loads()[2].wait()

    def dispatch(t, carry):
        q = lax.rem(t + GROUPS - 1, GROUPS)
        for c in range(PIECES):
            value = jnp.dot(pick[q], tok[:, c * CHUNK : (c + 1) * CHUNK], preferred_element_type=F32)
            to_stage(c, value.astype(BF16))
        pack(sent, q)

        @pl.when(t == 0)
        def _():
            pl.semaphore_wait(barrier, CHIPS)

        start = jnp.where(t == 0, SLOTS - 1 - EARLY, 0)
        send_some(sent, got, q, start, jnp.where(t == 0, SLOTS - 1, SLOTS), 1, there_send, there_recv)
        return carry

    lax.fori_loop(0, GROUPS, dispatch, 0)
    for copy in loads()[3:]:
        copy.start()
    send_some(sent, got, GROUPS - 1, 0, SLOTS - 1 - EARLY, 1, there_send, there_recv)
    keep_own(sent, got)
    for copy in loads()[3:]:
        copy.wait()

    def to_twin(source, target, send, recv):
        return pltpu.make_async_remote_copy(
            src_ref=source, dst_ref=target, send_sem=send, recv_sem=recv, device_id=twin, device_id_type=MESH
        )

    def over_rows(q):
        return to_twin(rows.at[q, pl.ds(0, OWN)], rows.at[q, pl.ds(OWN, OWN)], row_send.at[q], row_recv.at[q])

    def over_part(q, h):
        side = pl.ds(pl.multiple_of(h * HALF, HALF), HALF)
        return to_twin(part_out.at[q, :, side], part_in.at[q, :, side], part_send.at[SIDES * q + h], part_recv.at[SIDES * q + h])

    def arrive(q):
        wait_group(got, q, there_recv)

        def put(r, c, value):
            rows[q, r, c] = value

        unpack(got, q, put)
        over_rows(q).start()

    arrive(0)

    def work(q, carry):
        over_rows(q).wait_recv()

        def up(t, carry):
            lane = pl.ds(pl.multiple_of(t * 256, 256), 256)
            gate = jnp.dot(rows[q], w_gate[:, lane], preferred_element_type=F32)
            upper = jnp.dot(rows[q], w_up[:, lane], preferred_element_type=F32)
            hidden[:, lane] = (gate / (1.0 + jnp.exp(-gate)) * upper).astype(BF16)
            return carry

        lax.fori_loop(0, 3, up, 0)

        def side(h, carry):
            def down(t, carry):
                lane = pl.ds(pl.multiple_of(h * HALF + t * CHUNK, CHUNK), CHUNK)
                part = jnp.dot(hidden[...], w_down[:, lane], preferred_element_type=F32).astype(BF16)
                part_own[:, lane] = part[:OWN]
                part_out[q, :, lane] = part[OWN:]
                return carry

            lax.fori_loop(0, PIECES // SIDES, down, 0)
            over_part(q, h).start()
            return carry

        lax.fori_loop(0, SIDES, side, 0)

        @pl.when(q < GROUPS - 1)
        def _():
            arrive(q + 1)

        for c in range(PIECES):
            if c % (PIECES // SIDES) == 0:
                over_part(q, c // (PIECES // SIDES)).wait_recv()
            lane = slice(c * CHUNK, (c + 1) * CHUNK)
            to_stage(c, (part_own[:, lane].astype(F32) + part_in[q, :, lane].astype(F32)).astype(BF16))
        pack(answer, q)
        send_group(answer, back, q, -1, back_send, back_recv)
        return carry

    lax.fori_loop(0, GROUPS, work, 0)

    total[...] = jnp.zeros_like(total)

    def finish(q, put_sum):
        wait_group(back, q, back_recv)

        def put(r, c, value):
            flat[r, c] = value

        unpack(back, q, put)
        for c in range(PIECES):
            lane = slice(c * CHUNK, (c + 1) * CHUNK)
            high, low = (
                lax.dot_general(mixing[h, q], flat[:, lane], (((0,), (0,)), ((), ())), preferred_element_type=F32)
                for h in range(2)
            )
            put_sum(lane, total[:, lane] + high + low)

    def keep(lane, value):
        total[:, lane] = value

    def leave(lane, value):
        out[:, lane] = value.astype(BF16)

    def early(q, carry):
        finish(q, keep)
        return carry

    lax.fori_loop(0, GROUPS - 1, early, 0)
    finish(GROUPS - 1, leave)
    for q in range(GROUPS):
        over_rows(q).wait_send()
        for h in range(SIDES):
            over_part(q, h).wait_send()
    for source, send in ((sent, there_send), (answer, back_send)):
        ref = source.at[pl.ds(0, CHIPS - 1)]
        pltpu.make_async_copy(ref, ref, send).wait()


def body(tokens, expert_ids, gate_scores, w_gate, w_up, w_down):
    rows, width = tokens.shape
    half = w_gate.shape[2]
    blocks = (CHIPS, 2 * PIECES, LANES)
    m = 2 * SLOTS * PIECES
    vmem, hbm = pl.BlockSpec(memory_space=pltpu.VMEM), pl.BlockSpec(memory_space=pl.ANY)
    far = pl.BlockSpec(memory_space=pltpu.HBM)
    dma = pltpu.SemaphoreType.DMA
    return pl.pallas_call(
        kernel,
        out_shape=jax.ShapeDtypeStruct((rows, width), BF16),
        in_specs=[far, far, hbm, hbm, hbm, hbm],
        out_specs=vmem,
        scratch_shapes=[
            pltpu.VMEM(expert_ids.shape[::-1], jnp.int32),
            pltpu.VMEM(gate_scores.shape[::-1], F32),
            pltpu.VMEM((rows, width), BF16),
            pltpu.VMEM((width, half), BF16),
            pltpu.VMEM((width, half), BF16),
            pltpu.VMEM((half, width), BF16),
            pltpu.VMEM(blocks, BF16),
            pltpu.VMEM(blocks, BF16),
            pltpu.VMEM((GROUPS, 2 * OWN, width), BF16),
            pltpu.VMEM((2 * OWN, half), BF16),
            pltpu.VMEM((OWN, width), BF16),
            pltpu.VMEM((GROUPS, OWN, width), BF16),
            pltpu.VMEM((GROUPS, OWN, width), BF16),
            pltpu.VMEM(blocks, BF16),
            pltpu.VMEM(blocks, BF16),
            pltpu.VMEM((GROUPS, OWN, rows), BF16),
            pltpu.VMEM((2, GROUPS, OWN, rows), BF16),
            pltpu.VMEM((m, m), BF16),
            pltpu.VMEM((m, m), BF16),
            pltpu.VMEM((m, LANES), BF16),
            pltpu.VMEM((OWN, width), BF16),
            pltpu.VMEM((rows, width), F32),
            dma((6,)),
            dma, dma((GROUPS,)),
            dma((GROUPS,)), dma((GROUPS,)),
            dma((SIDES * GROUPS,)), dma((SIDES * GROUPS,)),
            dma, dma((GROUPS,)),
            dma,
        ],
        compiler_params=pltpu.CompilerParams(collective_id=0, has_side_effects=True, vmem_limit_bytes=52 << 20),
    )(expert_ids.T, gate_scores.T, tokens, w_gate, w_up, w_down)


def solution(mesh):
    split = ("group", "local")
    flat, deep = P(split, None), P(split, None, None)
    return jax.shard_map(
        body, mesh=mesh, in_specs=(flat, flat, flat, deep, deep, deep), out_specs=flat, check_vma=False
    )
```
